32 devices in a mesh: light: 8 (over y, x, core), tile: 4 (over z).
Axes of the slice: x: 2, y: 2, z: 4, core: 2. Of those that a mesh axis runs over, the one named last changes fastest.
Arguments:
- density: float32 [128, 32, 2048], P('light', 'tile'), may hold values from 0.03 to 9, as said below
- bin_index: int32 [128, 32, 2048], P('light', 'tile'), may hold values from 0 to 127
- transfer: float32 [4, 128], replicated, may hold values from 0.1 to 1
- depth_order: int32 [4], replicated, may hold values from 0 to 3, each once
Outputs:
- picture: float32 [4, 128, 2048], P(None, 'light', 'tile')
The draws below stay inside these ranges and needn't reach their ends.
Inputs may be any that keep to these rules, and one draw needn't show every extreme that they name: Positive density. `depth_order`: each rank of 0 to 3 once.
All inputs are finite; a program needn't handle non-finite values.
Results may differ from the reference program's by a relative error of at most 0.0003.
Values sent between devices are 32-bit elements; how exact they have to be, the bound alone decides.
No kernel may reach another device: no remote copies, remote signals or barrier semaphores. Data moves between devices by JAX's collectives and lax.ppermute only.
A program may use at most 256 MiB of HBM per device.

```python
import math
import jax
import jax.numpy as jnp
from jax import lax

CD = 8
NQ = 2048
NB = 128
NL = 128
ND = 32
DEPTH_SLABS = 4


def draw_density(key, part):
    first, second = jax.random.split(key)
    grain = jnp.exp(jax.random.uniform(first, (NL, ND, NQ), jnp.float32, math.log(0.3), math.log(3.0)))
    patches = jnp.exp(jax.random.uniform(second, (NL // 8, ND, NQ), jnp.float32, math.log(0.1), math.log(3.0)))
    return grain * jnp.repeat(patches, 8, axis=0)


def place_ends(drawn, stream_key, smallest, high):
    extent = drawn.shape
    index_at = [jax.random.randint(jax.random.fold_in(stream_key, axis), (), 0, extent[axis]) for axis in range(len(extent))]
    drawn = drawn.at[tuple(index_at)].set(smallest)
    longest = extent.index(max(extent))
    index_at[longest] = (index_at[longest] + 1) % extent[longest]
    return drawn.at[tuple(index_at)].set(high)


def setup_inputs(seed: int = 0) -> dict:
    key_of = jax.random.split(jax.random.key(seed), 5)
    density = draw_density(jax.random.fold_in(key_of[4], 71), 0)
    bin_index = place_ends(jax.random.randint(key_of[1], (NL, ND, NQ), 0, NB), jax.random.fold_in(key_of[1], 1), 0, NB - 1).astype(jnp.int32)
    transfer = jnp.clip(jnp.exp(jax.random.uniform(key_of[2], (4, NB), jnp.float32, math.log(0.1), math.log(1.0))), 0.1, 1.0)
    depth_order = jax.random.permutation(key_of[3], DEPTH_SLABS).astype(jnp.int32)
    return dict(density=density, bin_index=bin_index, transfer=transfer, depth_order=depth_order)


AMBIENT = 0.25


def reference(density, bin_index, transfer, depth_order):
    light_step = 3.0 / NL
    view_step = 3.0 / ND
    block_rows = 8
    inverse = jnp.argsort(depth_order).astype(jnp.int32)
    padded = jnp.pad(density, ((1, 1), (0, 0), (1, 1)))

    def view_order(field):
        return field.reshape(block_rows, DEPTH_SLABS, CD, NQ)[:, inverse].reshape(block_rows, ND, NQ)

    def render_block(upstream, block_index):
        row_start = (block_index * block_rows).astype(jnp.int32)
        window = lax.dynamic_slice_in_dim(padded, row_start, block_rows + 2, 0)
        cells = window[1:-1, :, 1:-1]
        grad_light = 0.5 * (window[2:, :, 1:-1] - window[:-2, :, 1:-1])
        grad_col = 0.5 * (window[1:-1, :, 2:] - window[1:-1, :, :-2])
        shading = 1.0 + 0.5 * jnp.tanh(grad_light + grad_col)
        entries = lax.dynamic_slice_in_dim(bin_index, row_start, block_rows, 0)
        looked = transfer[:, entries]
        extinction = looked[3] * cells
        running = jnp.cumsum(extinction, axis=0)
        light_depth = (upstream[None] + running - extinction) * light_step
        lighting = AMBIENT + jnp.exp(-light_depth) * shading
        view_depth = view_order(extinction) * view_step
        lit_view = view_order(lighting)
        ahead_depth = jnp.cumsum(view_depth, axis=1) - view_depth
        weight = jnp.exp(-ahead_depth) * (1.0 - jnp.exp(-view_depth))
        shaded = weight * lit_view
        emitted = jnp.stack([jnp.sum(shaded * view_order(looked[channel]), axis=1) for channel in range(3)])
        opacity = 1.0 - jnp.exp(-jnp.sum(view_depth, axis=1))
        result = jnp.concatenate([emitted, opacity[None]], axis=0)
        return upstream + running[-1], result

    start_plane = jnp.zeros((ND, NQ), jnp.float32)
    final_plane, blocks = lax.scan(render_block, start_plane, jnp.arange(NL // block_rows, dtype=jnp.int32))
    return blocks.transpose(1, 0, 2, 3).reshape(4, NL, NQ)
```

```python
import functools

import jax
import jax.numpy as jnp
from jax import lax
from jax.experimental import pallas as pl
from jax.experimental.pallas import tpu as pltpu
from jax.sharding import PartitionSpec as P

AMBIENT = 0.25
LANES = 128
VMEM = pltpu.VMEM
PARAMS = pltpu.CompilerParams(vmem_limit_bytes=48 * 2**20)


def full(memory_space=VMEM):
    return pl.BlockSpec(memory_space=memory_space)


def table_rows(table_ref, channel):
    entries = table_ref.shape[1]
    return [
        jnp.broadcast_to(table_ref[channel : channel + 1, first : first + LANES], (8, LANES))
        for first in range(0, entries, LANES)
    ]


def look_up(rows, index):
    low = index if len(rows) == 1 else index & (LANES - 1)
    value = jnp.take_along_axis(rows[0], low, axis=1)
    for part in range(1, len(rows)):
        value = jnp.where(index >= part * LANES, jnp.take_along_axis(rows[part], low, axis=1), value)
    return value


def extinction_kernel(density_ref, bin_ref, table_ref, ext_ref, before_ref, total_ref):
    light_cells, _, columns = density_ref.shape
    rows = table_rows(table_ref, 3)
    for first in range(0, columns, LANES):
        at = slice(first, first + LANES)
        running = jnp.zeros((8, LANES), jnp.float32)
        for i in range(light_cells):
            ext = look_up(rows, bin_ref[i, :, at]) * density_ref[i, :, at]
            ext_ref[first // LANES, 8 * i : 8 * i + 8] = ext
            before_ref[i, :, at] = running
            running = running + ext
        total_ref[:, at] = running


def local_kernel(
    light_step, view_step, ends_ref, density_ref, bin_ref, table_ref, ext_ref, before_ref, prev_ref, next_ref,
    lit_ref, ambient_ref, clear_ref, shade_ref, entry_ref,
):
    light_cells, depth_cells, columns = density_ref.shape
    lane = lax.broadcasted_iota(jnp.int32, (8, columns), 1)
    has_prev = ends_ref[0]
    has_next = ends_ref[1]

    def shade(i, above, below):
        cells = density_ref[i]
        right = jnp.where(lane == columns - 1, 0.0, pltpu.roll(cells, columns - 1, 1))
        left = jnp.where(lane == 0, 0.0, pltpu.roll(cells, 1, 1))
        slope = 0.5 * ((below - above) + (right - left))
        shading = 1.0 + 0.5 * jnp.tanh(slope)
        faded = jnp.exp(before_ref[i] * (-light_step)) * shading
        rows = pl.ds(pl.multiple_of(i * 8, 8), 8)
        for first in range(0, columns, LANES):
            at = slice(first, first + LANES)
            shade_ref[first // LANES, rows] = faded[:, at]
            entry_ref[first // LANES, rows] = bin_ref[i, :, at]

    shade(0, jnp.where(has_prev > 0, prev_ref[...], 0.0), density_ref[1])
    shade(
        light_cells - 1,
        density_ref[light_cells - 2],
        jnp.where(has_next > 0, next_ref[...], 0.0),
    )

    @pl.loop(1, light_cells - 1)
    def _(i):
        shade(i, density_ref[i - 1], density_ref[i + 1])

    tables = [table_rows(table_ref, c) for c in range(3)]

    @pl.loop(0, columns // LANES)
    def _(tile):
        at = pl.ds(pl.multiple_of(tile * LANES, LANES), LANES)
        for half in range(0, light_cells, 8):
            clear = jnp.ones((8, LANES), jnp.float32)
            ambient = [jnp.zeros((8, LANES), jnp.float32) for _ in range(3)]
            for j in range(depth_cells):
                cells = pl.ds(half * depth_cells + j, 8, stride=depth_cells)
                further = clear * jnp.exp(ext_ref[tile, cells] * (-view_step))
                weight = clear - further
                clear = further
                lit = weight * shade_ref[tile, cells]
                index = entry_ref[tile, cells]
                for c in range(3):
                    colour = look_up(tables[c], index)
                    lit_ref[c, j, half : half + 8, at] = lit * colour
                    ambient[c] = ambient[c] + weight * colour
            for c in range(3):
                ambient_ref[c, half : half + 8, at] = AMBIENT * ambient[c]
            clear_ref[half : half + 8, at] = clear


def picture_kernel(light_step, mine_ref, upstream_ref, lit_ref, ambient_ref, clear_ref, *refs):
    *out_refs, fade_ref = refs
    _, depth_cells, light_cells, columns = lit_ref.shape
    tiles = len(out_refs)
    share = columns // tiles
    fade_ref[...] = jnp.exp(upstream_ref[...] * (-light_step))
    for step, out_ref in enumerate(out_refs):
        owner = lax.rem(mine_ref[0] + step, tiles)
        for first in range(0, share, LANES):
            at = pl.ds(pl.multiple_of(owner * share + first, LANES), LANES)
            to = slice(first, first + LANES)
            for half in range(0, light_cells, 8):
                rows = slice(half, half + 8)
                sums = [ambient_ref[c, rows, at] for c in range(3)]
                for j in range(depth_cells):
                    fade = jnp.broadcast_to(fade_ref[j : j + 1, at], (8, LANES))
                    for c in range(3):
                        sums[c] = sums[c] + fade * lit_ref[c, j, rows, at]
                for c in range(3):
                    out_ref[c, rows, to] = sums[c]
                out_ref[3, rows, to] = clear_ref[rows, at]


def combine_kernel(mine_ref, order_ref, *refs):
    *in_refs, out_ref = refs
    tiles = len(in_refs)
    rank = [order_ref[lax.rem(mine_ref[0] - step + tiles, tiles)] for step in range(tiles)]
    clear = [ref[3] for ref in in_refs]
    colour = jnp.zeros(out_ref.shape[1:], jnp.float32)
    colour = [colour, colour, colour]
    through = jnp.ones_like(colour[0])
    for step in range(tiles):
        ahead = jnp.ones_like(through)
        for other in range(tiles):
            if other != step:
                ahead = ahead * jnp.where(rank[other] < rank[step], clear[other], 1.0)
        for c in range(3):
            colour[c] = colour[c] + ahead * in_refs[step][c]
        through = through * clear[step]
    for c in range(3):
        out_ref[c] = colour[c]
    out_ref[3] = 1.0 - through


def shape(*dims):
    return jax.ShapeDtypeStruct(dims, jnp.float32)


def per_device(density, bin_index, transfer, depth_order):
    light_cells, depth_cells, columns = density.shape
    light_count = lax.axis_size("light")
    tile_count = lax.axis_size("tile")
    light_mine = lax.axis_index("light")
    tile_mine = lax.axis_index("tile").astype(jnp.int32).reshape(1)
    light_step = 3.0 / (light_cells * light_count)
    view_step = 3.0 / (depth_cells * tile_count)
    share = columns // tile_count
    tiled = (columns // LANES, light_cells * depth_cells, LANES)

    ups = [(i, i + 1) for i in range(light_count - 1)]
    prev = lax.ppermute(density[-1], "light", ups)
    nxt = lax.ppermute(density[0], "light", [(b, a) for a, b in ups])

    ext, before, total = pl.pallas_call(
        extinction_kernel,
        out_shape=[shape(*tiled), shape(*density.shape), shape(depth_cells, columns)],
        in_specs=[full()] * 3,
        out_specs=[full()] * 3,
        compiler_params=PARAMS,
        name="extinction",
    )(density, bin_index, transfer)

    upstream = jnp.zeros_like(total)
    group = total
    step = 1
    while step < light_count:
        got = lax.ppermute(group, "light", [(i, i ^ step) for i in range(light_count)])
        upstream = upstream + jnp.where((light_mine & step) > 0, got, 0.0)
        group = group + got
        step *= 2

    ends = jnp.stack([light_mine > 0, light_mine < light_count - 1]).astype(jnp.int32)
    smem = full(pltpu.SMEM)
    lit, ambient, clear = pl.pallas_call(
        functools.partial(local_kernel, light_step, view_step),
        out_shape=[
            shape(3, depth_cells, light_cells, columns),
            shape(3, light_cells, columns),
            shape(light_cells, columns),
        ],
        in_specs=[smem] + [full()] * 7,
        out_specs=[full()] * 3,
        scratch_shapes=[pltpu.VMEM(tiled, jnp.float32), pltpu.VMEM(tiled, jnp.int32)],
        compiler_params=PARAMS,
        name="local",
    )(ends, density, bin_index, transfer, ext, before, prev, nxt)

    pieces = pl.pallas_call(
        functools.partial(picture_kernel, light_step),
        out_shape=[shape(4, light_cells, share)] * tile_count,
        in_specs=[smem] + [full()] * 4,
        out_specs=[full()] * tile_count,
        scratch_shapes=[pltpu.VMEM((depth_cells, columns), jnp.float32)],
        compiler_params=PARAMS,
        name="picture",
    )(tile_mine, upstream, lit, ambient, clear)

    held = [pieces[0]]
    for step in range(1, tile_count):
        held.append(
            lax.ppermute(pieces[step], "tile", [(i, (i + step) % tile_count) for i in range(tile_count)])
        )
    return pl.pallas_call(
        combine_kernel,
        out_shape=shape(4, light_cells, share),
        in_specs=[smem, smem] + [full()] * tile_count,
        out_specs=full(),
        compiler_params=PARAMS,
        name="combine",
    )(tile_mine, depth_order, *held)


def solution(mesh):
    in_specs = (P("light", "tile", None), P("light", "tile", None), P(), P())
    out_specs = P(None, "light", "tile")
    return jax.shard_map(
        per_device, mesh=mesh, in_specs=in_specs, out_specs=out_specs, check_vma=False
    )
```

```python
import functools

import jax
import jax.numpy as jnp
from jax import lax
from jax.experimental import pallas as pl
from jax.experimental.pallas import tpu as pltpu
from jax.sharding import PartitionSpec as P

AMBIENT = 0.25
LANES = 128
LOG2E = 1.4426950408889634
F32 = jnp.float32


def table_rows(table_ref, channel):
    entries = table_ref.shape[1]
    return [
        jnp.broadcast_to(table_ref[channel : channel + 1, first : first + LANES], (8, LANES))
        for first in range(0, entries, LANES)
    ]


def look_up(rows, index):
    low = index if len(rows) == 1 else index & (LANES - 1)
    value = jnp.take_along_axis(rows[0], low, axis=1)
    for part in range(1, len(rows)):
        value = jnp.where(index >= part * LANES, jnp.take_along_axis(rows[part], low, axis=1), value)
    return value


def lanes(tile):
    return slice(tile * LANES, (tile + 1) * LANES)


def eight(i):
    return pl.ds(pl.multiple_of(i * 8, 8), 8)


def extinction_kernel(
    tiles_along, density_hbm, bin_hbm, table_hbm, order_hbm,
    density_ref, table_ref, entry_ref, ext_ref, send_ref, edge_ref, front_ref,
    bin_ref, order_ref, density_sem, bin_sem, table_sem, order_sem,
):
    light_cells, _, columns = density_hbm.shape
    tiles = columns // LANES
    table_copy = pltpu.make_async_copy(table_hbm, table_ref, table_sem)
    table_copy.start()
    order_copy = pltpu.make_async_copy(order_hbm, order_ref, order_sem)
    order_copy.start()
    parts = 2
    size = light_cells // parts
    copies = []
    for part in range(parts):
        at = slice(part * size, (part + 1) * size)
        first = pltpu.make_async_copy(bin_hbm.at[at], bin_ref.at[at], bin_sem.at[part])
        second = pltpu.make_async_copy(density_hbm.at[at], density_ref.at[at], density_sem.at[part])
        first.start()
        second.start()
        copies.append((first, second))
    order_copy.wait()
    mine = lax.axis_index("tile")
    rank = [order_ref[lax.rem(mine - step + tiles_along, tiles_along)] for step in range(tiles_along)]
    for step in range(tiles_along):
        for other in range(tiles_along):
            front = jnp.where(rank[other] < rank[step], 1.0, 0.0)
            front_ref[step * tiles_along + other] = jnp.full((8, LANES), front, F32)
    table_copy.wait()
    rows = table_rows(table_ref, 3)
    running = tuple(jnp.zeros((8, LANES), F32) for _ in range(tiles))

    def layer(i, running):
        sums = []
        for tile in range(tiles):
            entry = bin_ref[i, :, lanes(tile)]
            ext = look_up(rows, entry) * density_ref[i, :, lanes(tile)]
            entry_ref[tile, eight(i)] = entry
            ext_ref[tile, eight(i)] = ext
            sums.append(running[tile] + ext)
        return tuple(sums)

    for part, (first, second) in enumerate(copies):
        first.wait()
        second.wait()
        running = lax.fori_loop(part * size, (part + 1) * size, layer, running, unroll=min(4, size))
    for tile in range(tiles):
        send_ref[0, :, lanes(tile)] = running[tile]
    odd = lax.rem(lax.axis_index("light"), 2)
    send_ref[1] = density_ref[(1 - odd) * (light_cells - 1)]
    edge_ref[...] = density_ref[odd * (light_cells - 1)]


def terms_kernel(view_step, table_ref, entry_ref, ext_ref, term_ref, clear_ref):
    _, depth_cells, light_cells, columns = term_ref.shape
    tables = [table_rows(table_ref, c) for c in range(3)]

    @pl.loop(0, columns // LANES, unroll=2)
    def _(tile):
        at = pl.ds(pl.multiple_of(tile * LANES, LANES), LANES)
        for half in range(0, light_cells, 8):
            clear = jnp.ones((8, LANES), F32)
            for j in range(depth_cells):
                cells = pl.ds(half * depth_cells + j, 8, stride=depth_cells)
                further = clear * jnp.exp2(ext_ref[tile, cells] * (-view_step * LOG2E))
                weight = clear - further
                clear = further
                entry = entry_ref[tile, cells]
                for c in range(3):
                    term_ref[c, j, half : half + 8, at] = weight * look_up(tables[c], entry)
            clear_ref[half : half + 8, at] = clear


def shade_kernel(light_step, density_ref, ext_ref, pair_ref, edge_ref, shade_ref):
    light_cells, _, columns = density_ref.shape
    odd = lax.rem(lax.axis_index("light"), 2) == 1
    lane = lax.broadcasted_iota(jnp.int32, (8, LANES), 1)
    zero = jnp.zeros((8, LANES), F32)
    count = columns // LANES

    def layer(i, before, above, below):
        after = []
        cells = [density_ref[i, :, lanes(tile)] for tile in range(count)]
        up = [pltpu.roll(value, 1, 1) for value in cells]
        down = [pltpu.roll(value, LANES - 1, 1) for value in cells]
        for tile in range(count):
            left = jnp.where(lane == 0, up[tile - 1] if tile else zero, up[tile])
            right = jnp.where(lane == LANES - 1, down[tile + 1] if tile < count - 1 else zero, down[tile])
            slope = 0.5 * ((below(tile) - above(tile)) + (right - left))
            fade = jnp.exp2(before[tile] * (-light_step * LOG2E))
            after.append(before[tile] + ext_ref[tile, eight(i)])
            shade_ref[tile, eight(i)] = fade * (1.0 + 0.5 * jnp.tanh(slope))
        return tuple(after)

    def inside(i):
        return lambda tile: density_ref[i, :, lanes(tile)]

    def outside(when_odd, when_even):
        return lambda tile: jnp.where(odd, when_odd(lanes(tile)), when_even(lanes(tile)))

    from_pair = lambda at: pair_ref[1, :, at]
    from_edge = lambda at: edge_ref[:, at]
    last = light_cells - 1
    before = layer(0, (zero,) * count, outside(from_pair, from_edge), inside(1))
    before = lax.fori_loop(1, last, lambda i, b: layer(i, b, inside(i - 1), inside(i + 1)), before, unroll=2)
    layer(last, before, inside(last - 1), outside(from_edge, from_pair))


def picture_kernel(light_step, tiles, shade_ref, term_ref, clear_ref, pair_ref, *refs):
    group_refs, out_refs, fade_ref = refs[: -tiles - 1], refs[-tiles - 1 : -1], refs[-1]
    _, depth_cells, light_cells, columns = term_ref.shape
    share = columns // tiles
    mine = lax.axis_index("tile")
    place = lax.axis_index("light")
    upstream = jnp.where((place & 1) > 0, pair_ref[0], 0.0)
    for level, group_ref in enumerate(group_refs):
        upstream = upstream + jnp.where((place & (2 << level)) > 0, group_ref[...], 0.0)
    fade_ref[...] = jnp.exp2(upstream * (-light_step * LOG2E))
    for step, out_ref in enumerate(out_refs):
        owner = lax.rem(mine + step, tiles)
        for tile in range(share // LANES):
            at = pl.ds(pl.multiple_of(owner * share + tile * LANES, LANES), LANES)
            for half in range(0, light_cells, 8):
                rows = slice(half, half + 8)
                sums = [jnp.zeros((8, LANES), F32) for _ in range(3)]
                for j in range(depth_cells):
                    fade = jnp.broadcast_to(fade_ref[j : j + 1, at], (8, LANES))
                    cells = pl.ds(half * depth_cells + j, 8, stride=depth_cells)
                    light = AMBIENT + fade * shade_ref[owner * (share // LANES) + tile, cells]
                    for c in range(3):
                        sums[c] = sums[c] + light * term_ref[c, j, rows, at]
                for c in range(3):
                    out_ref[c, rows, lanes(tile)] = sums[c]
                out_ref[3, rows, lanes(tile)] = clear_ref[rows, at]


def combine_kernel(front_ref, *refs):
    *in_refs, out_ref = refs
    steps = range(len(in_refs))
    _, light_cells, share = out_ref.shape
    for half in range(0, light_cells, 8):
        for tile in range(share // LANES):
            at = (slice(half, half + 8), lanes(tile))
            clear = [ref[3, *at] for ref in in_refs]
            sums = [jnp.zeros((8, LANES), F32) for _ in range(3)]
            through = clear[0]
            for step in steps[1:]:
                through = through * clear[step]
            for step in steps:
                ahead = jnp.ones((8, LANES), F32)
                for other in steps:
                    if other != step:
                        ahead = ahead * jnp.where(front_ref[step * len(steps) + other] > 0.5, clear[other], 1.0)
                for c in range(3):
                    sums[c] = sums[c] + ahead * in_refs[step][c, *at]
            for c in range(3):
                out_ref[c, *at] = sums[c]
            out_ref[3, *at] = 1.0 - through


def call(kernel, outs, ins, name, scratch=(), cost=1.0):
    cycles = int(cost * 1000)
    return pl.pallas_call(
        kernel,
        out_shape=outs,
        in_specs=[pl.BlockSpec(memory_space=pltpu.VMEM)] * len(ins),
        out_specs=jax.tree.map(lambda _: pl.BlockSpec(memory_space=pltpu.VMEM), outs),
        scratch_shapes=list(scratch),
        compiler_params=pltpu.CompilerParams(vmem_limit_bytes=8 * 2**20),
        cost_estimate=pl.CostEstimate(flops=cycles * 1000, bytes_accessed=cycles * 3000, transcendentals=0),
        name=name,
    )(*ins)


def per_device(density, bin_index, transfer, depth_order):
    light_cells, depth_cells, columns = density.shape
    light_count = lax.axis_size("light")
    tile_count = lax.axis_size("tile")
    light_step = 3.0 / (light_cells * light_count)
    view_step = 3.0 / (depth_cells * tile_count)
    share = columns // tile_count

    def shape(*dims, dtype=F32):
        return jax.ShapeDtypeStruct(dims, dtype)

    plane = shape(depth_cells, columns)
    tiled = (columns // LANES, light_cells * depth_cells, LANES)
    hbm = pl.BlockSpec(memory_space=pltpu.HBM)
    vmem = pl.BlockSpec(memory_space=pltpu.VMEM)
    outs = [
        shape(*density.shape), shape(*transfer.shape), shape(*tiled, dtype=jnp.int32), shape(*tiled),
        shape(2, *plane.shape), plane, shape(tile_count * tile_count, 8, LANES),
    ]
    dense, table, entry, ext, send, edge, front = pl.pallas_call(
        functools.partial(extinction_kernel, tile_count),
        out_shape=outs,
        in_specs=[hbm] * 4,
        out_specs=[vmem] * len(outs),
        scratch_shapes=[
            pltpu.VMEM(bin_index.shape, jnp.int32),
            pltpu.SMEM(depth_order.shape, jnp.int32),
            pltpu.SemaphoreType.DMA((2,)),
            pltpu.SemaphoreType.DMA((2,)),
            pltpu.SemaphoreType.DMA,
            pltpu.SemaphoreType.DMA,
        ],
        compiler_params=pltpu.CompilerParams(vmem_limit_bytes=8 * 2**20),
        name="extinction",
    )(*[pltpu.with_memory_space_constraint(a, pltpu.HBM) for a in (density, bin_index, transfer, depth_order)])

    pair = lax.ppermute(send, "light", [(i, i ^ 1) for i in range(light_count)])
    beside = [(i, i + 1) for i in range(1, light_count - 1, 2)]
    edge = lax.ppermute(edge, "light", beside + [(b, a) for a, b in beside])
    term, clear = call(
        functools.partial(terms_kernel, view_step),
        [shape(3, depth_cells, light_cells, columns), shape(light_cells, columns)],
        (table, entry, ext), "terms", cost=2.5,
    )
    shade = call(
        functools.partial(shade_kernel, light_step), shape(*tiled), (dense, ext, pair, edge), "shade", cost=1.2
    )
    group = send[0] + pair[0]
    groups = []
    step = 2
    while step < light_count:
        if step == light_count // 2:
            group, shade = lax.optimization_barrier((group, shade))
        got = lax.ppermute(group, "light", [(i, i ^ step) for i in range(light_count)])
        groups.append(got)
        group = group + got
        step *= 2
    pieces = call(
        functools.partial(picture_kernel, light_step, tile_count),
        [shape(4, light_cells, share)] * tile_count,
        (shade, term, clear, pair, *groups), "picture",
        scratch=[pltpu.VMEM(plane.shape, F32)], cost=0.6,
    )
    held = [pieces[0]]
    for step in range(1, tile_count):
        held.append(
            lax.ppermute(pieces[step], "tile", [(i, (i + step) % tile_count) for i in range(tile_count)])
        )
    return call(combine_kernel, shape(4, light_cells, share), (front, *held), "combine")


def solution(mesh):
    in_specs = (P("light", "tile", None), P("light", "tile", None), P(), P())
    out_specs = P(None, "light", "tile")
    return jax.shard_map(
        per_device, mesh=mesh, in_specs=in_specs, out_specs=out_specs, check_vma=False
    )
```

```python
import functools

import jax
import jax.numpy as jnp
from jax import lax
from jax.experimental import pallas as pl
from jax.experimental.pallas import tpu as pltpu
from jax.sharding import PartitionSpec as P

AMBIENT = 0.25
LANES = 128
LOG2E = 1.4426950408889634
F32 = jnp.float32


def table_rows(table_ref, channel):
    entries = table_ref.shape[1]
    return [
        jnp.broadcast_to(table_ref[channel : channel + 1, first : first + LANES], (8, LANES))
        for first in range(0, entries, LANES)
    ]


def look_up(rows, index):
    low = index if len(rows) == 1 else index & (LANES - 1)
    value = jnp.take_along_axis(rows[0], low, axis=1)
    for part in range(1, len(rows)):
        value = jnp.where(index >= part * LANES, jnp.take_along_axis(rows[part], low, axis=1), value)
    return value


def lanes(tile):
    return slice(tile * LANES, (tile + 1) * LANES)


def eight(i):
    return pl.ds(pl.multiple_of(i * 8, 8), 8)


def extinction_kernel(
    tiles_along, density_hbm, bin_hbm, table_hbm, order_hbm,
    density_ref, table_ref, entry_ref, ext_ref, send_ref, edge_ref, front_ref,
    bin_ref, order_ref, density_sem, bin_sem, table_sem, order_sem,
):
    light_cells, _, columns = density_hbm.shape
    tiles = columns // LANES
    table_copy = pltpu.make_async_copy(table_hbm, table_ref, table_sem)
    table_copy.start()
    order_copy = pltpu.make_async_copy(order_hbm, order_ref, order_sem)
    order_copy.start()
    parts = 2
    size = light_cells // parts
    copies = []
    for part in range(parts):
        at = slice(part * size, (part + 1) * size)
        first = pltpu.make_async_copy(bin_hbm.at[at], bin_ref.at[at], bin_sem.at[part])
        second = pltpu.make_async_copy(density_hbm.at[at], density_ref.at[at], density_sem.at[part])
        first.start()
        second.start()
        copies.append((first, second))
    order_copy.wait()
    mine = lax.axis_index("tile")
    rank = [order_ref[lax.rem(mine - step + tiles_along, tiles_along)] for step in range(tiles_along)]
    for step in range(tiles_along):
        for other in range(tiles_along):
            front = jnp.where(rank[other] < rank[step], 1.0, 0.0)
            front_ref[step * tiles_along + other] = jnp.full((8, LANES), front, F32)
    table_copy.wait()
    rows = table_rows(table_ref, 3)
    running = tuple(jnp.zeros((8, LANES), F32) for _ in range(tiles))

    def layer(i, running):
        sums = []
        for tile in range(tiles):
            entry = bin_ref[i, :, lanes(tile)]
            ext = look_up(rows, entry) * density_ref[i, :, lanes(tile)]
            entry_ref[tile, eight(i)] = entry
            ext_ref[tile, eight(i)] = ext
            sums.append(running[tile] + ext)
        return tuple(sums)

    for part, (first, second) in enumerate(copies):
        first.wait()
        second.wait()
        running = lax.fori_loop(part * size, (part + 1) * size, layer, running, unroll=min(4, size))
    for tile in range(tiles):
        send_ref[0, :, lanes(tile)] = running[tile]
    odd = lax.rem(lax.axis_index("light"), 2)
    send_ref[1] = density_ref[(1 - odd) * (light_cells - 1)]
    edge_ref[...] = density_ref[odd * (light_cells - 1)]


def terms_kernel(view_step, table_ref, entry_ref, ext_ref, term_ref, clear_ref):
    _, depth_cells, light_cells, columns = term_ref.shape
    tables = [table_rows(table_ref, c) for c in range(3)]

    @pl.loop(0, columns // LANES, unroll=2)
    def _(tile):
        at = pl.ds(pl.multiple_of(tile * LANES, LANES), LANES)
        for half in range(0, light_cells, 8):
            clear = jnp.ones((8, LANES), F32)
            for j in range(depth_cells):
                cells = pl.ds(half * depth_cells + j, 8, stride=depth_cells)
                further = clear * jnp.exp2(ext_ref[tile, cells] * (-view_step * LOG2E))
                weight = clear - further
                clear = further
                entry = entry_ref[tile, cells]
                for c in range(3):
                    term_ref[c, j, half : half + 8, at] = weight * look_up(tables[c], entry)
            clear_ref[half : half + 8, at] = clear


def shaded(light_step, cells, before, above, below):
    lane = lax.broadcasted_iota(jnp.int32, (8, LANES), 1)
    zero = jnp.zeros((8, LANES), F32)
    up = [pltpu.roll(value, 1, 1) for value in cells]
    down = [pltpu.roll(value, LANES - 1, 1) for value in cells]
    result = []
    for tile in range(len(cells)):
        left = jnp.where(lane == 0, up[tile - 1] if tile else zero, up[tile])
        right = jnp.where(lane == LANES - 1, down[tile + 1] if tile < len(cells) - 1 else zero, down[tile])
        slope = 0.5 * ((below(tile) - above(tile)) + (right - left))
        fade = jnp.exp2(before[tile] * (-light_step * LOG2E))
        result.append(fade * (1.0 + 0.5 * jnp.tanh(slope)))
    return result


def shade_kernel(light_step, density_ref, ext_ref, shade_ref):
    light_cells, _, columns = density_ref.shape
    count = columns // LANES

    def layer(i, before):
        values = shaded(
            light_step,
            [density_ref[i, :, lanes(tile)] for tile in range(count)],
            before,
            lambda tile: density_ref[i - 1, :, lanes(tile)],
            lambda tile: density_ref[i + 1, :, lanes(tile)],
        )
        for tile in range(count):
            shade_ref[tile, eight(i)] = values[tile]
        return tuple(before[tile] + ext_ref[tile, eight(i)] for tile in range(count))

    for tile in range(count):
        shade_ref[tile, eight(0)] = jnp.zeros((8, LANES), F32)
        shade_ref[tile, eight(light_cells - 1)] = jnp.zeros((8, LANES), F32)
    before = tuple(ext_ref[tile, eight(0)] for tile in range(count))
    lax.fori_loop(1, light_cells - 1, layer, before, unroll=2)


def outer_kernel(light_step, light_count, density_ref, ext_ref, send_ref, pair_ref, edge_ref, _, shade_ref):
    light_cells, _, columns = density_ref.shape
    count = columns // LANES
    place = lax.axis_index("light")
    odd = lax.rem(place, 2) == 1
    inner = jnp.logical_and(place > 0, place < light_count - 1)
    last = light_cells - 1

    def beside(tile, pair_here):
        edge = jnp.where(inner, edge_ref[:, lanes(tile)], 0.0)
        return jnp.where(pair_here, pair_ref[1, :, lanes(tile)], edge)

    zero = jnp.zeros((8, LANES), F32)
    first = shaded(
        light_step, [density_ref[0, :, lanes(tile)] for tile in range(count)], [zero] * count,
        lambda tile: beside(tile, odd),
        lambda tile: density_ref[1, :, lanes(tile)],
    )
    for tile in range(count):
        shade_ref[tile, 0:8] = first[tile]
    final = shaded(
        light_step, [density_ref[last, :, lanes(tile)] for tile in range(count)],
        [send_ref[0, :, lanes(tile)] - ext_ref[tile, last * 8 : last * 8 + 8] for tile in range(count)],
        lambda tile: density_ref[last - 1, :, lanes(tile)],
        lambda tile: beside(tile, jnp.logical_not(odd)),
    )
    for tile in range(count):
        shade_ref[tile, last * 8 : last * 8 + 8] = final[tile]


def picture_kernel(light_step, tiles, shade_ref, term_ref, clear_ref, pair_ref, *refs):
    group_refs, out_refs, fade_ref = refs[: -tiles - 1], refs[-tiles - 1 : -1], refs[-1]
    _, depth_cells, light_cells, columns = term_ref.shape
    share = columns // tiles
    mine = lax.axis_index("tile")
    place = lax.axis_index("light")
    upstream = jnp.where((place & 1) > 0, pair_ref[0], 0.0)
    for level, group_ref in enumerate(group_refs):
        upstream = upstream + jnp.where((place & (2 << level)) > 0, group_ref[...], 0.0)
    fade_ref[...] = jnp.exp2(upstream * (-light_step * LOG2E))
    for step, out_ref in enumerate(out_refs):
        owner = lax.rem(mine + step, tiles)
        for tile in range(share // LANES):
            at = pl.ds(pl.multiple_of(owner * share + tile * LANES, LANES), LANES)
            for half in range(0, light_cells, 8):
                rows = slice(half, half + 8)
                sums = [jnp.zeros((8, LANES), F32) for _ in range(3)]
                for j in range(depth_cells):
                    fade = jnp.broadcast_to(fade_ref[j : j + 1, at], (8, LANES))
                    cells = pl.ds(half * depth_cells + j, 8, stride=depth_cells)
                    light = AMBIENT + fade * shade_ref[owner * (share // LANES) + tile, cells]
                    for c in range(3):
                        sums[c] = sums[c] + light * term_ref[c, j, rows, at]
                for c in range(3):
                    out_ref[c, rows, lanes(tile)] = sums[c]
                out_ref[3, rows, lanes(tile)] = clear_ref[rows, at]


def combine_kernel(front_ref, *refs):
    *in_refs, out_ref = refs
    steps = range(len(in_refs))
    _, light_cells, share = out_ref.shape
    for half in range(0, light_cells, 8):
        for tile in range(share // LANES):
            at = (slice(half, half + 8), lanes(tile))
            clear = [ref[3, *at] for ref in in_refs]
            sums = [jnp.zeros((8, LANES), F32) for _ in range(3)]
            through = clear[0]
            for step in steps[1:]:
                through = through * clear[step]
            for step in steps:
                ahead = jnp.ones((8, LANES), F32)
                for other in steps:
                    if other != step:
                        ahead = ahead * jnp.where(front_ref[step * len(steps) + other] > 0.5, clear[other], 1.0)
                for c in range(3):
                    sums[c] = sums[c] + ahead * in_refs[step][c, *at]
            for c in range(3):
                out_ref[c, *at] = sums[c]
            out_ref[3, *at] = 1.0 - through


def call(kernel, outs, ins, name, scratch=(), cost=1.0, aliases=None):
    cycles = int(cost * 1000)
    return pl.pallas_call(
        kernel,
        out_shape=outs,
        in_specs=[pl.BlockSpec(memory_space=pltpu.VMEM)] * len(ins),
        out_specs=jax.tree.map(lambda _: pl.BlockSpec(memory_space=pltpu.VMEM), outs),
        scratch_shapes=list(scratch),
        compiler_params=pltpu.CompilerParams(vmem_limit_bytes=8 * 2**20),
        cost_estimate=pl.CostEstimate(flops=cycles * 1000, bytes_accessed=cycles * 3000, transcendentals=0),
        input_output_aliases=aliases or {},
        name=name,
    )(*ins)


def per_device(density, bin_index, transfer, depth_order):
    light_cells, depth_cells, columns = density.shape
    light_count = lax.axis_size("light")
    tile_count = lax.axis_size("tile")
    light_step = 3.0 / (light_cells * light_count)
    view_step = 3.0 / (depth_cells * tile_count)
    share = columns // tile_count

    def shape(*dims, dtype=F32):
        return jax.ShapeDtypeStruct(dims, dtype)

    plane = shape(depth_cells, columns)
    tiled = (columns // LANES, light_cells * depth_cells, LANES)
    hbm = pl.BlockSpec(memory_space=pltpu.HBM)
    vmem = pl.BlockSpec(memory_space=pltpu.VMEM)
    outs = [
        shape(*density.shape), shape(*transfer.shape), shape(*tiled, dtype=jnp.int32), shape(*tiled),
        shape(2, *plane.shape), plane, shape(tile_count * tile_count, 8, LANES),
    ]
    dense, table, entry, ext, send, edge, front = pl.pallas_call(
        functools.partial(extinction_kernel, tile_count),
        out_shape=outs,
        in_specs=[hbm] * 4,
        out_specs=[vmem] * len(outs),
        scratch_shapes=[
            pltpu.VMEM(bin_index.shape, jnp.int32),
            pltpu.SMEM(depth_order.shape, jnp.int32),
            pltpu.SemaphoreType.DMA((2,)),
            pltpu.SemaphoreType.DMA((2,)),
            pltpu.SemaphoreType.DMA,
            pltpu.SemaphoreType.DMA,
        ],
        compiler_params=pltpu.CompilerParams(vmem_limit_bytes=8 * 2**20),
        name="extinction",
    )(*[pltpu.with_memory_space_constraint(a, pltpu.HBM) for a in (density, bin_index, transfer, depth_order)])

    pair = lax.ppermute(send, "light", [(i, i ^ 1) for i in range(light_count)])
    beside = [(i, (i + 1) % light_count) for i in range(1, light_count, 2)]
    edge = lax.ppermute(edge, "light", beside + [(b, a) for a, b in beside])
    term, clear = call(
        functools.partial(terms_kernel, view_step),
        [shape(3, depth_cells, light_cells, columns), shape(light_cells, columns)],
        (table, entry, ext), "terms", cost=2.5,
    )
    shade = call(
        functools.partial(shade_kernel, light_step), shape(*tiled), (dense, ext), "shade", cost=1.2
    )
    group = send[0] + pair[0]
    groups = []
    step = 2
    while step < light_count:
        if step == light_count // 2:
            group, shade = lax.optimization_barrier((group, shade))
        got = lax.ppermute(group, "light", [(i, i ^ step) for i in range(light_count)])
        groups.append(got)
        group = group + got
        step *= 2
    shade = call(
        functools.partial(outer_kernel, light_step, light_count), shape(*tiled),
        (dense, ext, send, pair, edge, shade), "outer", cost=0.2, aliases={5: 0},
    )
    pieces = call(
        functools.partial(picture_kernel, light_step, tile_count),
        [shape(4, light_cells, share)] * tile_count,
        (shade, term, clear, pair, *groups), "picture",
        scratch=[pltpu.VMEM(plane.shape, F32)], cost=0.6,
    )
    held = [pieces[0]]
    for step in range(1, tile_count):
        held.append(
            lax.ppermute(pieces[step], "tile", [(i, (i + step) % tile_count) for i in range(tile_count)])
        )
    return call(combine_kernel, shape(4, light_cells, share), (front, *held), "combine")


def solution(mesh):
    in_specs = (P("light", "tile", None), P("light", "tile", None), P(), P())
    out_specs = P(None, "light", "tile")
    return jax.shard_map(
        per_device, mesh=mesh, in_specs=in_specs, out_specs=out_specs, check_vma=False
    )
```

```python
import functools

import jax
import jax.numpy as jnp
from jax import lax
from jax.experimental import pallas as pl
from jax.experimental.pallas import tpu as pltpu
from jax.sharding import PartitionSpec as P

AMBIENT = 0.25
LANES = 128
LOG2E = 1.4426950408889634
F32 = jnp.float32


def table_rows(table_ref, channel):
    entries = table_ref.shape[1]
    return [
        jnp.broadcast_to(table_ref[channel : channel + 1, first : first + LANES], (8, LANES))
        for first in range(0, entries, LANES)
    ]


def look_up(rows, index):
    low = index if len(rows) == 1 else index & (LANES - 1)
    value = jnp.take_along_axis(rows[0], low, axis=1)
    for part in range(1, len(rows)):
        value = jnp.where(index >= part * LANES, jnp.take_along_axis(rows[part], low, axis=1), value)
    return value


def lanes(tile):
    return slice(tile * LANES, (tile + 1) * LANES)


def eight(i):
    return pl.ds(pl.multiple_of(i * 8, 8), 8)


def extinction_kernel(
    tiles_along, density_hbm, bin_hbm, table_hbm, order_hbm,
    density_ref, table_ref, entry_ref, ext_ref, send_ref, edge_ref, front_ref,
    bin_ref, order_ref, density_sem, bin_sem, table_sem, order_sem,
):
    light_cells, _, columns = density_hbm.shape
    tiles = columns // LANES
    table_copy = pltpu.make_async_copy(table_hbm, table_ref, table_sem)
    table_copy.start()
    order_copy = pltpu.make_async_copy(order_hbm, order_ref, order_sem)
    order_copy.start()
    parts = 2
    size = light_cells // parts
    copies = []
    for part in range(parts):
        at = slice(part * size, (part + 1) * size)
        first = pltpu.make_async_copy(bin_hbm.at[at], bin_ref.at[at], bin_sem.at[part])
        second = pltpu.make_async_copy(density_hbm.at[at], density_ref.at[at], density_sem.at[part])
        first.start()
        second.start()
        copies.append((first, second))
    order_copy.wait()
    mine = lax.axis_index("tile")
    rank = [order_ref[lax.rem(mine - step + tiles_along, tiles_along)] for step in range(tiles_along)]
    for step in range(tiles_along):
        for other in range(tiles_along):
            front = jnp.where(rank[other] < rank[step], 1.0, 0.0)
            front_ref[step * tiles_along + other] = jnp.full((8, LANES), front, F32)
    table_copy.wait()
    rows = table_rows(table_ref, 3)
    running = tuple(jnp.zeros((8, LANES), F32) for _ in range(tiles))

    def layer(i, running):
        sums = []
        for tile in range(tiles):
            entry = bin_ref[i, :, lanes(tile)]
            ext = look_up(rows, entry) * density_ref[i, :, lanes(tile)]
            entry_ref[tile, eight(i)] = entry
            ext_ref[tile, eight(i)] = ext
            sums.append(running[tile] + ext)
        return tuple(sums)

    for part, (first, second) in enumerate(copies):
        first.wait()
        second.wait()
        running = lax.fori_loop(part * size, (part + 1) * size, layer, running, unroll=min(4, size))
    for tile in range(tiles):
        send_ref[0, :, lanes(tile)] = running[tile]
    odd = lax.rem(lax.axis_index("light"), 2)
    send_ref[1] = density_ref[(1 - odd) * (light_cells - 1)]
    edge_ref[...] = density_ref[odd * (light_cells - 1)]


def terms_kernel(view_step, table_ref, entry_ref, ext_ref, term_ref, clear_ref):
    _, depth_cells, light_cells, columns = term_ref.shape
    tables = [table_rows(table_ref, c) for c in range(3)]

    @pl.loop(0, columns // LANES, unroll=4)
    def _(tile):
        at = pl.ds(pl.multiple_of(tile * LANES, LANES), LANES)
        for half in range(0, light_cells, 8):
            clear = jnp.ones((8, LANES), F32)
            for j in range(depth_cells):
                cells = pl.ds(half * depth_cells + j, 8, stride=depth_cells)
                further = clear * jnp.exp2(ext_ref[tile, cells] * (-view_step * LOG2E))
                weight = clear - further
                clear = further
                entry = entry_ref[tile, cells]
                for c in range(3):
                    term_ref[c, j, half : half + 8, at] = weight * look_up(tables[c], entry)
            clear_ref[half : half + 8, at] = clear


def shaded(light_step, cells, before, above, below):
    lane = lax.broadcasted_iota(jnp.int32, (8, LANES), 1)
    zero = jnp.zeros((8, LANES), F32)
    up = [pltpu.roll(value, 1, 1) for value in cells]
    down = [pltpu.roll(value, LANES - 1, 1) for value in cells]
    result = []
    for tile in range(len(cells)):
        left = jnp.where(lane == 0, up[tile - 1] if tile else zero, up[tile])
        right = jnp.where(lane == LANES - 1, down[tile + 1] if tile < len(cells) - 1 else zero, down[tile])
        slope = 0.5 * ((below(tile) - above(tile)) + (right - left))
        fade = jnp.exp2(before[tile] * (-light_step * LOG2E))
        result.append(fade * (1.0 + 0.5 * jnp.tanh(slope)))
    return result


def shade_kernel(light_step, density_ref, ext_ref, shade_ref):
    light_cells, _, columns = density_ref.shape
    count = columns // LANES

    def layer(i, before):
        values = shaded(
            light_step,
            [density_ref[i, :, lanes(tile)] for tile in range(count)],
            before,
            lambda tile: density_ref[i - 1, :, lanes(tile)],
            lambda tile: density_ref[i + 1, :, lanes(tile)],
        )
        for tile in range(count):
            shade_ref[tile, eight(i)] = values[tile]
        return tuple(before[tile] + ext_ref[tile, eight(i)] for tile in range(count))

    for tile in range(count):
        shade_ref[tile, eight(0)] = jnp.zeros((8, LANES), F32)
        shade_ref[tile, eight(light_cells - 1)] = jnp.zeros((8, LANES), F32)
    before = tuple(ext_ref[tile, eight(0)] for tile in range(count))
    lax.fori_loop(1, light_cells - 1, layer, before, unroll=2)


def outer_kernel(light_step, light_count, density_ref, ext_ref, send_ref, pair_ref, edge_ref, _, shade_ref):
    light_cells, _, columns = density_ref.shape
    count = columns // LANES
    place = lax.axis_index("light")
    odd = lax.rem(place, 2) == 1
    inner = jnp.logical_and(place > 0, place < light_count - 1)
    last = light_cells - 1

    def beside(tile, pair_here):
        edge = jnp.where(inner, edge_ref[:, lanes(tile)], 0.0)
        return jnp.where(pair_here, pair_ref[1, :, lanes(tile)], edge)

    zero = jnp.zeros((8, LANES), F32)
    first = shaded(
        light_step, [density_ref[0, :, lanes(tile)] for tile in range(count)], [zero] * count,
        lambda tile: beside(tile, odd),
        lambda tile: density_ref[1, :, lanes(tile)],
    )
    for tile in range(count):
        shade_ref[tile, 0:8] = first[tile]
    final = shaded(
        light_step, [density_ref[last, :, lanes(tile)] for tile in range(count)],
        [send_ref[0, :, lanes(tile)] - ext_ref[tile, last * 8 : last * 8 + 8] for tile in range(count)],
        lambda tile: density_ref[last - 1, :, lanes(tile)],
        lambda tile: beside(tile, jnp.logical_not(odd)),
    )
    for tile in range(count):
        shade_ref[tile, last * 8 : last * 8 + 8] = final[tile]


def picture_kernel(light_step, tiles, masks, shade_ref, term_ref, clear_ref, pair_ref, *refs):
    group_refs, out_refs, fade_ref = refs[: -tiles - 1], refs[-tiles - 1 : -1], refs[-1]
    _, depth_cells, light_cells, columns = term_ref.shape
    share = columns // tiles
    mine = lax.axis_index("tile")
    place = lax.axis_index("light")
    upstream = jnp.where((place & 1) > 0, pair_ref[0], 0.0)
    for mask, group_ref in zip(masks, group_refs):
        upstream = upstream + jnp.where((place ^ mask) < place, group_ref[...], 0.0)
    fade_ref[...] = jnp.exp2(upstream * (-light_step * LOG2E))
    for step, out_ref in enumerate(out_refs):
        owner = lax.rem(mine + step, tiles)
        for tile in range(share // LANES):
            at = pl.ds(pl.multiple_of(owner * share + tile * LANES, LANES), LANES)
            for half in range(0, light_cells, 8):
                rows = slice(half, half + 8)
                sums = [jnp.zeros((8, LANES), F32) for _ in range(3)]
                for j in range(depth_cells):
                    fade = jnp.broadcast_to(fade_ref[j : j + 1, at], (8, LANES))
                    cells = pl.ds(half * depth_cells + j, 8, stride=depth_cells)
                    light = AMBIENT + fade * shade_ref[owner * (share // LANES) + tile, cells]
                    for c in range(3):
                        sums[c] = sums[c] + light * term_ref[c, j, rows, at]
                for c in range(3):
                    out_ref[c, rows, lanes(tile)] = sums[c]
                out_ref[3, rows, lanes(tile)] = clear_ref[rows, at]


def combine_kernel(front_ref, *refs):
    *in_refs, out_ref = refs
    steps = range(len(in_refs))
    _, light_cells, share = out_ref.shape
    for half in range(0, light_cells, 8):
        for tile in range(share // LANES):
            at = (slice(half, half + 8), lanes(tile))
            clear = [ref[3, *at] for ref in in_refs]
            sums = [jnp.zeros((8, LANES), F32) for _ in range(3)]
            through = clear[0]
            for step in steps[1:]:
                through = through * clear[step]
            for step in steps:
                ahead = jnp.ones((8, LANES), F32)
                for other in steps:
                    if other != step:
                        ahead = ahead * jnp.where(front_ref[step * len(steps) + other] > 0.5, clear[other], 1.0)
                for c in range(3):
                    sums[c] = sums[c] + ahead * in_refs[step][c, *at]
            for c in range(3):
                out_ref[c, *at] = sums[c]
            out_ref[3, *at] = 1.0 - through


def call(kernel, outs, ins, name, scratch=(), cost=1.0, aliases=None):
    cycles = int(cost * 1000)
    return pl.pallas_call(
        kernel,
        out_shape=outs,
        in_specs=[pl.BlockSpec(memory_space=pltpu.VMEM)] * len(ins),
        out_specs=jax.tree.map(lambda _: pl.BlockSpec(memory_space=pltpu.VMEM), outs),
        scratch_shapes=list(scratch),
        compiler_params=pltpu.CompilerParams(vmem_limit_bytes=8 * 2**20),
        cost_estimate=pl.CostEstimate(flops=cycles * 1000, bytes_accessed=cycles * 3000, transcendentals=0),
        input_output_aliases=aliases or {},
        name=name,
    )(*ins)


def per_device(density, bin_index, transfer, depth_order):
    light_cells, depth_cells, columns = density.shape
    light_count = lax.axis_size("light")
    tile_count = lax.axis_size("tile")
    light_step = 3.0 / (light_cells * light_count)
    view_step = 3.0 / (depth_cells * tile_count)
    share = columns // tile_count

    def shape(*dims, dtype=F32):
        return jax.ShapeDtypeStruct(dims, dtype)

    plane = shape(depth_cells, columns)
    tiled = (columns // LANES, light_cells * depth_cells, LANES)
    hbm = pl.BlockSpec(memory_space=pltpu.HBM)
    vmem = pl.BlockSpec(memory_space=pltpu.VMEM)
    outs = [
        shape(*density.shape), shape(*transfer.shape), shape(*tiled, dtype=jnp.int32), shape(*tiled),
        shape(2, *plane.shape), plane, shape(tile_count * tile_count, 8, LANES),
    ]
    dense, table, entry, ext, send, edge, front = pl.pallas_call(
        functools.partial(extinction_kernel, tile_count),
        out_shape=outs,
        in_specs=[hbm] * 4,
        out_specs=[vmem] * len(outs),
        scratch_shapes=[
            pltpu.VMEM(bin_index.shape, jnp.int32),
            pltpu.SMEM(depth_order.shape, jnp.int32),
            pltpu.SemaphoreType.DMA((2,)),
            pltpu.SemaphoreType.DMA((2,)),
            pltpu.SemaphoreType.DMA,
            pltpu.SemaphoreType.DMA,
        ],
        compiler_params=pltpu.CompilerParams(vmem_limit_bytes=8 * 2**20),
        name="extinction",
    )(*[pltpu.with_memory_space_constraint(a, pltpu.HBM) for a in (density, bin_index, transfer, depth_order)])

    pair = lax.ppermute(send, "light", [(i, i ^ 1) for i in range(light_count)])
    beside = [(i, (i + 1) % light_count) for i in range(1, light_count, 2)]
    edge = lax.ppermute(edge, "light", beside + [(b, a) for a, b in beside])
    term, clear = call(
        functools.partial(terms_kernel, view_step),
        [shape(3, depth_cells, light_cells, columns), shape(light_cells, columns)],
        (table, entry, ext), "terms", cost=2.5,
    )
    shade = call(
        functools.partial(shade_kernel, light_step), shape(*tiled), (dense, ext), "shade", cost=1.2
    )
    group = send[0] + pair[0]
    groups = []
    masks = []
    step = 2
    while step < light_count:
        reach = [m * step for m in (1, 2, 3)] if step * 4 <= light_count else [step]
        got = [lax.ppermute(group, "light", [(i, i ^ m) for i in range(light_count)]) for m in reach]
        groups += got
        masks += reach
        group = group + functools.reduce(jnp.add, got)
        step *= len(reach) + 1
    shade = call(
        functools.partial(outer_kernel, light_step, light_count), shape(*tiled),
        (dense, ext, send, pair, edge, shade), "outer", cost=0.2, aliases={5: 0},
    )
    pieces = call(
        functools.partial(picture_kernel, light_step, tile_count, masks),
        [shape(4, light_cells, share)] * tile_count,
        (shade, term, clear, pair, *groups), "picture",
        scratch=[pltpu.VMEM(plane.shape, F32)], cost=0.6,
    )
    held = [pieces[0]]
    for step in range(1, tile_count):
        held.append(
            lax.ppermute(pieces[step], "tile", [(i, (i + step) % tile_count) for i in range(tile_count)])
        )
    return call(combine_kernel, shape(4, light_cells, share), (front, *held), "combine")


def solution(mesh):
    in_specs = (P("light", "tile", None), P("light", "tile", None), P(), P())
    out_specs = P(None, "light", "tile")
    return jax.shard_map(
        per_device, mesh=mesh, in_specs=in_specs, out_specs=out_specs, check_vma=False
    )
```

```python
import functools

import jax
import jax.numpy as jnp
from jax import lax
from jax.experimental import pallas as pl
from jax.experimental.pallas import tpu as pltpu
from jax.sharding import PartitionSpec as P

AMBIENT = 0.25
LANES = 128
LOG2E = 1.4426950408889634
F32 = jnp.float32


def table_rows(table_ref, channel):
    entries = table_ref.shape[1]
    return [
        jnp.broadcast_to(table_ref[channel : channel + 1, first : first + LANES], (8, LANES))
        for first in range(0, entries, LANES)
    ]


def look_up(rows, index):
    low = index if len(rows) == 1 else index & (LANES - 1)
    value = jnp.take_along_axis(rows[0], low, axis=1)
    for part in range(1, len(rows)):
        value = jnp.where(index >= part * LANES, jnp.take_along_axis(rows[part], low, axis=1), value)
    return value


def lanes(tile):
    return slice(tile * LANES, (tile + 1) * LANES)


def eight(i):
    return pl.ds(pl.multiple_of(i * 8, 8), 8)


def extinction_kernel(
    tiles_along, density_hbm, bin_hbm, table_hbm, order_hbm,
    density_ref, table_ref, entry_ref, ext_ref, send_ref, edge_ref, front_ref,
    bin_ref, order_ref, density_sem, bin_sem, table_sem, order_sem,
):
    light_cells, _, columns = density_hbm.shape
    tiles = columns // LANES
    table_copy = pltpu.make_async_copy(table_hbm, table_ref, table_sem)
    table_copy.start()
    order_copy = pltpu.make_async_copy(order_hbm, order_ref, order_sem)
    order_copy.start()
    parts = 2
    size = light_cells // parts
    copies = []
    for part in range(parts):
        at = slice(part * size, (part + 1) * size)
        first = pltpu.make_async_copy(bin_hbm.at[at], bin_ref.at[at], bin_sem.at[part])
        second = pltpu.make_async_copy(density_hbm.at[at], density_ref.at[at], density_sem.at[part])
        first.start()
        second.start()
        copies.append((first, second))
    order_copy.wait()
    mine = lax.axis_index("tile")
    rank = [order_ref[lax.rem(mine - step + tiles_along, tiles_along)] for step in range(tiles_along)]
    for step in range(tiles_along):
        for other in range(tiles_along):
            front = jnp.where(rank[other] < rank[step], 1.0, 0.0)
            front_ref[step * tiles_along + other] = jnp.full((8, LANES), front, F32)
    table_copy.wait()
    rows = table_rows(table_ref, 3)
    running = tuple(jnp.zeros((8, LANES), F32) for _ in range(tiles))

    def layer(i, running):
        sums = []
        for tile in range(tiles):
            entry = bin_ref[i, :, lanes(tile)]
            ext = look_up(rows, entry) * density_ref[i, :, lanes(tile)]
            entry_ref[tile, eight(i)] = entry
            ext_ref[tile, eight(i)] = ext
            sums.append(running[tile] + ext)
        return tuple(sums)

    for part, (first, second) in enumerate(copies):
        first.wait()
        second.wait()
        running = lax.fori_loop(part * size, (part + 1) * size, layer, running, unroll=size)
    for tile in range(tiles):
        send_ref[0, :, lanes(tile)] = running[tile]
    odd = lax.rem(lax.axis_index("light"), 2)
    send_ref[1] = density_ref[(1 - odd) * (light_cells - 1)]
    edge_ref[...] = density_ref[odd * (light_cells - 1)]


def terms_kernel(view_step, table_ref, entry_ref, ext_ref, term_ref, clear_ref):
    _, depth_cells, light_cells, columns = term_ref.shape
    tables = [table_rows(table_ref, c) for c in range(3)]

    @pl.loop(0, columns // LANES, unroll=4)
    def _(tile):
        at = pl.ds(pl.multiple_of(tile * LANES, LANES), LANES)
        for half in range(0, light_cells, 8):
            clear = jnp.ones((8, LANES), F32)
            for j in range(depth_cells):
                cells = pl.ds(half * depth_cells + j, 8, stride=depth_cells)
                further = clear * jnp.exp2(ext_ref[tile, cells] * (-view_step * LOG2E))
                weight = clear - further
                clear = further
                entry = entry_ref[tile, cells]
                for c in range(3):
                    term_ref[c, j, half : half + 8, at] = weight * look_up(tables[c], entry)
            clear_ref[half : half + 8, at] = clear


def shaded(light_step, cells, before, above, below):
    lane = lax.broadcasted_iota(jnp.int32, (8, LANES), 1)
    zero = jnp.zeros((8, LANES), F32)
    up = [pltpu.roll(value, 1, 1) for value in cells]
    down = [pltpu.roll(value, LANES - 1, 1) for value in cells]
    result = []
    for tile in range(len(cells)):
        left = jnp.where(lane == 0, up[tile - 1] if tile else zero, up[tile])
        right = jnp.where(lane == LANES - 1, down[tile + 1] if tile < len(cells) - 1 else zero, down[tile])
        slope = 0.5 * ((below(tile) - above(tile)) + (right - left))
        fade = jnp.exp2(before[tile] * (-light_step * LOG2E))
        result.append(fade * (1.0 + 0.5 * jnp.tanh(slope)))
    return result


def shade_kernel(light_step, density_ref, ext_ref, shade_ref):
    light_cells, _, columns = density_ref.shape
    count = columns // LANES

    def layer(i, before):
        values = shaded(
            light_step,
            [density_ref[i, :, lanes(tile)] for tile in range(count)],
            before,
            lambda tile: density_ref[i - 1, :, lanes(tile)],
            lambda tile: density_ref[i + 1, :, lanes(tile)],
        )
        for tile in range(count):
            shade_ref[tile, eight(i)] = values[tile]
        return tuple(before[tile] + ext_ref[tile, eight(i)] for tile in range(count))

    for tile in range(count):
        shade_ref[tile, eight(0)] = jnp.zeros((8, LANES), F32)
        shade_ref[tile, eight(light_cells - 1)] = jnp.zeros((8, LANES), F32)
    before = tuple(ext_ref[tile, eight(0)] for tile in range(count))
    lax.fori_loop(1, light_cells - 1, layer, before, unroll=2)


def outer_kernel(light_step, light_count, density_ref, ext_ref, send_ref, pair_ref, edge_ref, _, shade_ref):
    light_cells, _, columns = density_ref.shape
    count = columns // LANES
    place = lax.axis_index("light")
    odd = lax.rem(place, 2) == 1
    inner = jnp.logical_and(place > 0, place < light_count - 1)
    last = light_cells - 1

    def beside(tile, pair_here):
        edge = jnp.where(inner, edge_ref[:, lanes(tile)], 0.0)
        return jnp.where(pair_here, pair_ref[1, :, lanes(tile)], edge)

    zero = jnp.zeros((8, LANES), F32)
    first = shaded(
        light_step, [density_ref[0, :, lanes(tile)] for tile in range(count)], [zero] * count,
        lambda tile: beside(tile, odd),
        lambda tile: density_ref[1, :, lanes(tile)],
    )
    for tile in range(count):
        shade_ref[tile, 0:8] = first[tile]
    final = shaded(
        light_step, [density_ref[last, :, lanes(tile)] for tile in range(count)],
        [send_ref[0, :, lanes(tile)] - ext_ref[tile, last * 8 : last * 8 + 8] for tile in range(count)],
        lambda tile: density_ref[last - 1, :, lanes(tile)],
        lambda tile: beside(tile, jnp.logical_not(odd)),
    )
    for tile in range(count):
        shade_ref[tile, last * 8 : last * 8 + 8] = final[tile]


def picture_kernel(light_step, tiles, masks, steps, shade_ref, term_ref, clear_ref, pair_ref, *refs):
    group_refs, out_refs, fade_ref = refs[: -len(steps) - 1], refs[-len(steps) - 1 : -1], refs[-1]
    _, depth_cells, light_cells, columns = term_ref.shape
    share = columns // tiles
    mine = lax.axis_index("tile")
    place = lax.axis_index("light")
    upstream = jnp.where((place & 1) > 0, pair_ref[0], 0.0)
    for mask, group_ref in zip(masks, group_refs):
        upstream = upstream + jnp.where((place ^ mask) < place, group_ref[...], 0.0)
    fade_ref[...] = jnp.exp2(upstream * (-light_step * LOG2E))
    for step, out_ref in zip(steps, out_refs):
        owner = lax.rem(mine + step, tiles)
        for tile in range(share // LANES):
            at = pl.ds(pl.multiple_of(owner * share + tile * LANES, LANES), LANES)
            for half in range(0, light_cells, 8):
                rows = slice(half, half + 8)
                sums = [jnp.zeros((8, LANES), F32) for _ in range(3)]
                for j in range(depth_cells):
                    fade = jnp.broadcast_to(fade_ref[j : j + 1, at], (8, LANES))
                    cells = pl.ds(half * depth_cells + j, 8, stride=depth_cells)
                    light = AMBIENT + fade * shade_ref[owner * (share // LANES) + tile, cells]
                    for c in range(3):
                        sums[c] = sums[c] + light * term_ref[c, j, rows, at]
                for c in range(3):
                    out_ref[c, rows, lanes(tile)] = sums[c]
                out_ref[3, rows, lanes(tile)] = clear_ref[rows, at]


def combine_kernel(front_ref, *refs):
    *in_refs, out_ref = refs
    steps = range(len(in_refs))
    _, light_cells, share = out_ref.shape
    for half in range(0, light_cells, 8):
        for tile in range(share // LANES):
            at = (slice(half, half + 8), lanes(tile))
            clear = [ref[3, *at] for ref in in_refs]
            sums = [jnp.zeros((8, LANES), F32) for _ in range(3)]
            through = clear[0]
            for step in steps[1:]:
                through = through * clear[step]
            for step in steps:
                ahead = jnp.ones((8, LANES), F32)
                for other in steps:
                    if other != step:
                        ahead = ahead * jnp.where(front_ref[step * len(steps) + other] > 0.5, clear[other], 1.0)
                for c in range(3):
                    sums[c] = sums[c] + ahead * in_refs[step][c, *at]
            for c in range(3):
                out_ref[c, *at] = sums[c]
            out_ref[3, *at] = 1.0 - through


def call(kernel, outs, ins, name, scratch=(), cost=1.0, aliases=None):
    cycles = int(cost * 1000)
    return pl.pallas_call(
        kernel,
        out_shape=outs,
        in_specs=[pl.BlockSpec(memory_space=pltpu.VMEM)] * len(ins),
        out_specs=jax.tree.map(lambda _: pl.BlockSpec(memory_space=pltpu.VMEM), outs),
        scratch_shapes=list(scratch),
        compiler_params=pltpu.CompilerParams(vmem_limit_bytes=8 * 2**20),
        cost_estimate=pl.CostEstimate(flops=cycles * 1000, bytes_accessed=cycles * 3000, transcendentals=0),
        input_output_aliases=aliases or {},
        name=name,
    )(*ins)


def per_device(density, bin_index, transfer, depth_order):
    light_cells, depth_cells, columns = density.shape
    light_count = lax.axis_size("light")
    tile_count = lax.axis_size("tile")
    light_step = 3.0 / (light_cells * light_count)
    view_step = 3.0 / (depth_cells * tile_count)
    share = columns // tile_count

    def shape(*dims, dtype=F32):
        return jax.ShapeDtypeStruct(dims, dtype)

    plane = shape(depth_cells, columns)
    tiled = (columns // LANES, light_cells * depth_cells, LANES)
    hbm = pl.BlockSpec(memory_space=pltpu.HBM)
    vmem = pl.BlockSpec(memory_space=pltpu.VMEM)
    outs = [
        shape(*density.shape), shape(*transfer.shape), shape(*tiled, dtype=jnp.int32), shape(*tiled),
        shape(2, *plane.shape), plane, shape(tile_count * tile_count, 8, LANES),
    ]
    dense, table, entry, ext, send, edge, front = pl.pallas_call(
        functools.partial(extinction_kernel, tile_count),
        out_shape=outs,
        in_specs=[hbm] * 4,
        out_specs=[vmem] * len(outs),
        scratch_shapes=[
            pltpu.VMEM(bin_index.shape, jnp.int32),
            pltpu.SMEM(depth_order.shape, jnp.int32),
            pltpu.SemaphoreType.DMA((2,)),
            pltpu.SemaphoreType.DMA((2,)),
            pltpu.SemaphoreType.DMA,
            pltpu.SemaphoreType.DMA,
        ],
        compiler_params=pltpu.CompilerParams(vmem_limit_bytes=8 * 2**20),
        name="extinction",
    )(*[pltpu.with_memory_space_constraint(a, pltpu.HBM) for a in (density, bin_index, transfer, depth_order)])

    pair = lax.ppermute(send, "light", [(i, i ^ 1) for i in range(light_count)])
    beside = [(i, (i + 1) % light_count) for i in range(1, light_count, 2)]
    edge = lax.ppermute(edge, "light", beside + [(b, a) for a, b in beside])
    term, clear = call(
        functools.partial(terms_kernel, view_step),
        [shape(3, depth_cells, light_cells, columns), shape(light_cells, columns)],
        (table, entry, ext), "terms", cost=2.5,
    )
    shade = call(
        functools.partial(shade_kernel, light_step), shape(*tiled), (dense, ext), "shade", cost=1.2
    )
    group = send[0] + pair[0]
    groups = []
    masks = []
    step = 2
    while step < light_count:
        reach = [m * step for m in (1, 2, 3)] if step * 4 <= light_count else [step]
        got = [lax.ppermute(group, "light", [(i, i ^ m) for i in range(light_count)]) for m in reach]
        groups += got
        masks += reach
        group = group + functools.reduce(jnp.add, got)
        step *= len(reach) + 1
    shade = call(
        functools.partial(outer_kernel, light_step, light_count), shape(*tiled),
        (dense, ext, send, pair, edge, shade), "outer", cost=0.2, aliases={5: 0},
    )
    held = {}
    for steps in ([1], [*range(2, tile_count), 0]):
        pieces = call(
            functools.partial(picture_kernel, light_step, tile_count, masks, steps),
            [shape(4, light_cells, share)] * len(steps),
            (shade, term, clear, pair, *groups), "picture",
            scratch=[pltpu.VMEM(plane.shape, F32)], cost=0.2 * len(steps),
        )
        for step, piece in zip(steps, pieces):
            held[step] = piece
            if step:
                held[step] = lax.ppermute(piece, "tile", [(i, (i + step) % tile_count) for i in range(tile_count)])
    return call(
        combine_kernel, shape(4, light_cells, share), (front, *[held[step] for step in range(tile_count)]), "combine"
    )


def solution(mesh):
    in_specs = (P("light", "tile", None), P("light", "tile", None), P(), P())
    out_specs = P(None, "light", "tile")
    return jax.shard_map(
        per_device, mesh=mesh, in_specs=in_specs, out_specs=out_specs, check_vma=False
    )
```

```python
import functools

import jax
import jax.numpy as jnp
from jax import lax
from jax.experimental import pallas as pl
from jax.experimental.pallas import tpu as pltpu
from jax.sharding import PartitionSpec as P

AMBIENT = 0.25
LANES = 128
LOG2E = 1.4426950408889634
F32 = jnp.float32


def table_rows(table_ref, channel):
    entries = table_ref.shape[1]
    return [
        jnp.broadcast_to(table_ref[channel : channel + 1, first : first + LANES], (8, LANES))
        for first in range(0, entries, LANES)
    ]


def look_up(rows, index):
    low = index if len(rows) == 1 else index & (LANES - 1)
    value = jnp.take_along_axis(rows[0], low, axis=1)
    for part in range(1, len(rows)):
        value = jnp.where(index >= part * LANES, jnp.take_along_axis(rows[part], low, axis=1), value)
    return value


def lanes(tile):
    return slice(tile * LANES, (tile + 1) * LANES)


def eight(i):
    return pl.ds(pl.multiple_of(i * 8, 8), 8)


def extinction_kernel(
    tiles_along, density_hbm, bin_hbm, table_hbm, order_hbm,
    density_ref, bin_ref, table_ref, ext_ref, send_ref, edge_ref, front_ref,
    order_ref, density_sem, bin_sem, table_sem, order_sem,
):
    light_cells, _, columns = density_hbm.shape
    tiles = columns // LANES
    table_copy = pltpu.make_async_copy(table_hbm, table_ref, table_sem)
    table_copy.start()
    order_copy = pltpu.make_async_copy(order_hbm, order_ref, order_sem)
    order_copy.start()
    parts = 2
    size = light_cells // parts
    copies = []
    for part in range(parts):
        at = slice(part * size, (part + 1) * size)
        first = pltpu.make_async_copy(bin_hbm.at[at], bin_ref.at[at], bin_sem.at[part])
        second = pltpu.make_async_copy(density_hbm.at[at], density_ref.at[at], density_sem.at[part])
        first.start()
        second.start()
        copies.append((first, second))
    order_copy.wait()
    mine = lax.axis_index("tile")
    rank = [order_ref[lax.rem(mine - step + tiles_along, tiles_along)] for step in range(tiles_along)]
    for step in range(tiles_along):
        for other in range(tiles_along):
            front = jnp.where(rank[other] < rank[step], 1.0, 0.0)
            front_ref[step * tiles_along + other] = jnp.full((8, LANES), front, F32)
    table_copy.wait()
    rows = table_rows(table_ref, 3)
    running = tuple(jnp.zeros((8, LANES), F32) for _ in range(tiles))

    def layer(i, running):
        sums = []
        for tile in range(tiles):
            entry = bin_ref[i, :, lanes(tile)]
            ext = look_up(rows, entry) * density_ref[i, :, lanes(tile)]
            ext_ref[tile, eight(i)] = ext
            sums.append(running[tile] + ext)
        return tuple(sums)

    for part, (first, second) in enumerate(copies):
        first.wait()
        second.wait()
        running = lax.fori_loop(part * size, (part + 1) * size, layer, running, unroll=size)
    for tile in range(tiles):
        send_ref[0, :, lanes(tile)] = running[tile]
    odd = lax.rem(lax.axis_index("light"), 2)
    send_ref[1] = density_ref[(1 - odd) * (light_cells - 1)]
    edge_ref[...] = density_ref[odd * (light_cells - 1)]


def terms_kernel(view_step, table_ref, entry_ref, ext_ref, term_ref, clear_ref):
    _, depth_cells, light_cells, columns = term_ref.shape
    tables = [table_rows(table_ref, c) for c in range(3)]

    @pl.loop(0, columns // LANES, unroll=8)
    def _(tile):
        at = pl.ds(pl.multiple_of(tile * LANES, LANES), LANES)
        for half in range(0, light_cells, 8):
            clear = jnp.ones((8, LANES), F32)
            for j in range(depth_cells):
                cells = pl.ds(half * depth_cells + j, 8, stride=depth_cells)
                further = clear * jnp.exp2(ext_ref[tile, cells] * (-view_step * LOG2E))
                weight = clear - further
                clear = further
                entry = entry_ref[tile, cells]
                for c in range(3):
                    term_ref[c, j, half : half + 8, at] = weight * look_up(tables[c], entry)
            clear_ref[half : half + 8, at] = clear


def shaded(light_step, cells, before, above, below):
    lane = lax.broadcasted_iota(jnp.int32, (8, LANES), 1)
    zero = jnp.zeros((8, LANES), F32)
    up = [pltpu.roll(value, 1, 1) for value in cells]
    down = [pltpu.roll(value, LANES - 1, 1) for value in cells]
    result = []
    for tile in range(len(cells)):
        left = jnp.where(lane == 0, up[tile - 1] if tile else zero, up[tile])
        right = jnp.where(lane == LANES - 1, down[tile + 1] if tile < len(cells) - 1 else zero, down[tile])
        slope = 0.5 * ((below(tile) - above(tile)) + (right - left))
        fade = jnp.exp2(before[tile] * (-light_step * LOG2E))
        result.append(fade * (1.0 + 0.5 * jnp.tanh(slope)))
    return result


def shade_kernel(light_step, density_ref, bin_ref, ext_ref, shade_ref, entry_ref):
    light_cells, _, columns = density_ref.shape
    count = columns // LANES

    def layer(i, before):
        values = shaded(
            light_step,
            [density_ref[i, :, lanes(tile)] for tile in range(count)],
            before,
            lambda tile: density_ref[i - 1, :, lanes(tile)],
            lambda tile: density_ref[i + 1, :, lanes(tile)],
        )
        for tile in range(count):
            shade_ref[tile, eight(i)] = values[tile]
            entry_ref[tile, eight(i)] = bin_ref[i, :, lanes(tile)]
        return tuple(before[tile] + ext_ref[tile, eight(i)] for tile in range(count))

    for tile in range(count):
        shade_ref[tile, eight(0)] = jnp.zeros((8, LANES), F32)
        shade_ref[tile, eight(light_cells - 1)] = jnp.zeros((8, LANES), F32)
        for i in (0, light_cells - 1):
            entry_ref[tile, eight(i)] = bin_ref[i, :, lanes(tile)]
    before = tuple(ext_ref[tile, eight(0)] for tile in range(count))
    lax.fori_loop(1, light_cells - 1, layer, before, unroll=7)


def outer_kernel(light_step, light_count, density_ref, ext_ref, send_ref, pair_ref, edge_ref, _, shade_ref):
    light_cells, _, columns = density_ref.shape
    count = columns // LANES
    place = lax.axis_index("light")
    odd = lax.rem(place, 2) == 1
    inner = jnp.logical_and(place > 0, place < light_count - 1)
    last = light_cells - 1

    def beside(tile, pair_here):
        edge = jnp.where(inner, edge_ref[:, lanes(tile)], 0.0)
        return jnp.where(pair_here, pair_ref[1, :, lanes(tile)], edge)

    zero = jnp.zeros((8, LANES), F32)
    first = shaded(
        light_step, [density_ref[0, :, lanes(tile)] for tile in range(count)], [zero] * count,
        lambda tile: beside(tile, odd),
        lambda tile: density_ref[1, :, lanes(tile)],
    )
    for tile in range(count):
        shade_ref[tile, 0:8] = first[tile]
    final = shaded(
        light_step, [density_ref[last, :, lanes(tile)] for tile in range(count)],
        [send_ref[0, :, lanes(tile)] - ext_ref[tile, last * 8 : last * 8 + 8] for tile in range(count)],
        lambda tile: density_ref[last - 1, :, lanes(tile)],
        lambda tile: beside(tile, jnp.logical_not(odd)),
    )
    for tile in range(count):
        shade_ref[tile, last * 8 : last * 8 + 8] = final[tile]


def picture_kernel(light_step, tiles, masks, steps, shade_ref, term_ref, clear_ref, pair_ref, *refs):
    group_refs, out_refs, fade_ref = refs[: -len(steps) - 1], refs[-len(steps) - 1 : -1], refs[-1]
    _, depth_cells, light_cells, columns = term_ref.shape
    share = columns // tiles
    mine = lax.axis_index("tile")
    place = lax.axis_index("light")
    upstream = jnp.where((place & 1) > 0, pair_ref[0], 0.0)
    for (even, odd), group_ref in zip(masks, group_refs):
        source = place ^ jnp.where((place & 1) > 0, odd, even)
        upstream = upstream + jnp.where(source < place, group_ref[...], 0.0)
    fade_ref[...] = jnp.exp2(upstream * (-light_step * LOG2E))
    for step, out_ref in zip(steps, out_refs):
        owner = lax.rem(mine + step, tiles)
        for tile in range(share // LANES):
            at = pl.ds(pl.multiple_of(owner * share + tile * LANES, LANES), LANES)
            for half in range(0, light_cells, 8):
                rows = slice(half, half + 8)
                sums = [jnp.zeros((8, LANES), F32) for _ in range(3)]
                for j in range(depth_cells):
                    fade = jnp.broadcast_to(fade_ref[j : j + 1, at], (8, LANES))
                    cells = pl.ds(half * depth_cells + j, 8, stride=depth_cells)
                    light = AMBIENT + fade * shade_ref[owner * (share // LANES) + tile, cells]
                    for c in range(3):
                        sums[c] = sums[c] + light * term_ref[c, j, rows, at]
                for c in range(3):
                    out_ref[c, rows, lanes(tile)] = sums[c]
                out_ref[3, rows, lanes(tile)] = clear_ref[rows, at]


def combine_kernel(front_ref, *refs):
    *in_refs, out_ref = refs
    steps = range(len(in_refs))
    _, light_cells, share = out_ref.shape
    for half in range(0, light_cells, 8):
        for tile in range(share // LANES):
            at = (slice(half, half + 8), lanes(tile))
            clear = [ref[3, *at] for ref in in_refs]
            sums = [jnp.zeros((8, LANES), F32) for _ in range(3)]
            through = clear[0]
            for step in steps[1:]:
                through = through * clear[step]
            for step in steps:
                ahead = jnp.ones((8, LANES), F32)
                for other in steps:
                    if other != step:
                        ahead = ahead * jnp.where(front_ref[step * len(steps) + other] > 0.5, clear[other], 1.0)
                for c in range(3):
                    sums[c] = sums[c] + ahead * in_refs[step][c, *at]
            for c in range(3):
                out_ref[c, *at] = sums[c]
            out_ref[3, *at] = 1.0 - through


def call(kernel, outs, ins, name, scratch=(), cost=1.0, aliases=None):
    cycles = int(cost * 1000)
    return pl.pallas_call(
        kernel,
        out_shape=outs,
        in_specs=[pl.BlockSpec(memory_space=pltpu.VMEM)] * len(ins),
        out_specs=jax.tree.map(lambda _: pl.BlockSpec(memory_space=pltpu.VMEM), outs),
        scratch_shapes=list(scratch),
        compiler_params=pltpu.CompilerParams(vmem_limit_bytes=8 * 2**20),
        cost_estimate=pl.CostEstimate(flops=cycles * 1000, bytes_accessed=cycles * 3000, transcendentals=0),
        input_output_aliases=aliases or {},
        name=name,
    )(*ins)


def per_device(density, bin_index, transfer, depth_order):
    light_cells, depth_cells, columns = density.shape
    light_count = lax.axis_size("light")
    tile_count = lax.axis_size("tile")
    light_step = 3.0 / (light_cells * light_count)
    view_step = 3.0 / (depth_cells * tile_count)
    share = columns // tile_count

    def shape(*dims, dtype=F32):
        return jax.ShapeDtypeStruct(dims, dtype)

    plane = shape(depth_cells, columns)
    tiled = (columns // LANES, light_cells * depth_cells, LANES)
    hbm = pl.BlockSpec(memory_space=pltpu.HBM)
    vmem = pl.BlockSpec(memory_space=pltpu.VMEM)
    outs = [
        shape(*density.shape), shape(*density.shape, dtype=jnp.int32), shape(*transfer.shape), shape(*tiled),
        shape(2, *plane.shape), plane, shape(tile_count * tile_count, 8, LANES),
    ]
    dense, bins, table, ext, send, edge, front = pl.pallas_call(
        functools.partial(extinction_kernel, tile_count),
        out_shape=outs,
        in_specs=[hbm] * 4,
        out_specs=[vmem] * len(outs),
        scratch_shapes=[
            pltpu.SMEM(depth_order.shape, jnp.int32),
            pltpu.SemaphoreType.DMA((2,)),
            pltpu.SemaphoreType.DMA((2,)),
            pltpu.SemaphoreType.DMA,
            pltpu.SemaphoreType.DMA,
        ],
        compiler_params=pltpu.CompilerParams(vmem_limit_bytes=8 * 2**20),
        name="extinction",
    )(*[pltpu.with_memory_space_constraint(a, pltpu.HBM) for a in (density, bin_index, transfer, depth_order)])

    pair = lax.ppermute(send, "light", [(i, i ^ 1) for i in range(light_count)])
    beside = [(i, (i + 1) % light_count) for i in range(1, light_count, 2)]
    edge = lax.ppermute(edge, "light", beside + [(b, a) for a, b in beside])
    shade, entry = call(
        functools.partial(shade_kernel, light_step), [shape(*tiled), shape(*tiled, dtype=jnp.int32)],
        (dense, bins, ext), "shade", cost=1.2,
    )
    term, clear = call(
        functools.partial(terms_kernel, view_step),
        [shape(3, depth_cells, light_cells, columns), shape(light_cells, columns)],
        (table, entry, ext), "terms", cost=2.5,
    )
    group = send[0] + pair[0]
    groups = []
    masks = []
    step = 2
    while step < light_count:
        reach = [(a * step, b * step) for a, b in ((1, 2), (2, 1), (3, 3))] if step * 4 <= light_count else [(step, step)]
        got = [
            lax.ppermute(group, "light", [(i, i ^ masks_of[i % 2]) for i in range(light_count)]) for masks_of in reach
        ]
        groups += got
        masks += reach
        group = group + functools.reduce(jnp.add, got)
        step *= len(reach) + 1
    shade = call(
        functools.partial(outer_kernel, light_step, light_count), shape(*tiled),
        (dense, ext, send, pair, edge, shade), "outer", cost=0.2, aliases={5: 0},
    )
    held = {}
    for steps in ([1], [*range(2, tile_count), 0]):
        pieces = call(
            functools.partial(picture_kernel, light_step, tile_count, masks, steps),
            [shape(4, light_cells, share)] * len(steps),
            (shade, term, clear, pair, *groups), "picture",
            scratch=[pltpu.VMEM(plane.shape, F32)], cost=0.2 * len(steps),
        )
        for step, piece in zip(steps, pieces):
            held[step] = piece
            if step:
                held[step] = lax.ppermute(piece, "tile", [(i, (i + step) % tile_count) for i in range(tile_count)])
    return call(
        combine_kernel, shape(4, light_cells, share), (front, *[held[step] for step in range(tile_count)]), "combine"
    )


def solution(mesh):
    in_specs = (P("light", "tile", None), P("light", "tile", None), P(), P())
    out_specs = P(None, "light", "tile")
    return jax.shard_map(
        per_device, mesh=mesh, in_specs=in_specs, out_specs=out_specs, check_vma=False
    )
```

```python
import functools

import jax
import jax.numpy as jnp
from jax import lax
from jax.experimental import pallas as pl
from jax.experimental.pallas import tpu as pltpu
from jax.sharding import PartitionSpec as P

AMBIENT = 0.25
LANES = 128
LOG2E = 1.4426950408889634
F32 = jnp.float32


def table_rows(table_ref, channel):
    entries = table_ref.shape[1]
    return [
        jnp.broadcast_to(table_ref[channel : channel + 1, first : first + LANES], (8, LANES))
        for first in range(0, entries, LANES)
    ]


def look_up(rows, index):
    low = index if len(rows) == 1 else index & (LANES - 1)
    value = jnp.take_along_axis(rows[0], low, axis=1)
    for part in range(1, len(rows)):
        value = jnp.where(index >= part * LANES, jnp.take_along_axis(rows[part], low, axis=1), value)
    return value


def lanes(tile):
    return slice(tile * LANES, (tile + 1) * LANES)


def eight(i):
    return pl.ds(pl.multiple_of(i * 8, 8), 8)


def extinction_kernel(
    tiles_along, density_hbm, bin_hbm, table_hbm, order_hbm,
    density_ref, table_ref, entry_ref, ext_ref, send_ref, edge_ref, front_ref,
    bin_ref, order_ref, density_sem, bin_sem, table_sem, order_sem,
):
    light_cells, _, columns = density_hbm.shape
    tiles = columns // LANES
    table_copy = pltpu.make_async_copy(table_hbm, table_ref, table_sem)
    table_copy.start()
    order_copy = pltpu.make_async_copy(order_hbm, order_ref, order_sem)
    order_copy.start()
    parts = 2
    size = light_cells // parts
    copies = []
    for part in range(parts):
        at = slice(part * size, (part + 1) * size)
        first = pltpu.make_async_copy(bin_hbm.at[at], bin_ref.at[at], bin_sem.at[part])
        second = pltpu.make_async_copy(density_hbm.at[at], density_ref.at[at], density_sem.at[part])
        first.start()
        second.start()
        copies.append((first, second))
    order_copy.wait()
    mine = lax.axis_index("tile")
    rank = [order_ref[lax.rem(mine - step + tiles_along, tiles_along)] for step in range(tiles_along)]
    for step in range(tiles_along):
        for other in range(tiles_along):
            front = jnp.where(rank[other] < rank[step], 1.0, 0.0)
            front_ref[step * tiles_along + other] = jnp.full((8, LANES), front, F32)
    table_copy.wait()
    rows = table_rows(table_ref, 3)
    running = tuple(jnp.zeros((8, LANES), F32) for _ in range(tiles))

    def layer(i, running):
        sums = []
        for tile in range(tiles):
            entry = bin_ref[i, :, lanes(tile)]
            ext = look_up(rows, entry) * density_ref[i, :, lanes(tile)]
            entry_ref[tile, eight(i)] = entry
            ext_ref[tile, eight(i)] = ext
            sums.append(running[tile] + ext)
        return tuple(sums)

    for part, (first, second) in enumerate(copies):
        first.wait()
        second.wait()
        running = lax.fori_loop(part * size, (part + 1) * size, layer, running, unroll=size)
    for tile in range(tiles):
        send_ref[0, :, lanes(tile)] = running[tile]
    odd = lax.rem(lax.axis_index("light"), 2)
    send_ref[1] = density_ref[(1 - odd) * (light_cells - 1)]
    edge_ref[...] = density_ref[odd * (light_cells - 1)]


def terms_kernel(view_step, table_ref, entry_ref, ext_ref, term_ref, clear_ref):
    _, depth_cells, light_cells, columns = term_ref.shape
    tables = [table_rows(table_ref, c) for c in range(3)]

    @pl.loop(0, columns // LANES, unroll=4)
    def _(tile):
        at = pl.ds(pl.multiple_of(tile * LANES, LANES), LANES)
        for half in range(0, light_cells, 8):
            clear = jnp.ones((8, LANES), F32)
            for j in range(depth_cells):
                cells = pl.ds(half * depth_cells + j, 8, stride=depth_cells)
                further = clear * jnp.exp2(ext_ref[tile, cells] * (-view_step * LOG2E))
                weight = clear - further
                clear = further
                entry = entry_ref[tile, cells]
                for c in range(3):
                    term_ref[c, j, half : half + 8, at] = weight * look_up(tables[c], entry)
            clear_ref[half : half + 8, at] = clear


def shaded(light_step, cells, before, above, below):
    lane = lax.broadcasted_iota(jnp.int32, (8, LANES), 1)
    zero = jnp.zeros((8, LANES), F32)
    up = [pltpu.roll(value, 1, 1) for value in cells]
    down = [pltpu.roll(value, LANES - 1, 1) for value in cells]
    result = []
    for tile in range(len(cells)):
        left = jnp.where(lane == 0, up[tile - 1] if tile else zero, up[tile])
        right = jnp.where(lane == LANES - 1, down[tile + 1] if tile < len(cells) - 1 else zero, down[tile])
        slope = 0.5 * ((below(tile) - above(tile)) + (right - left))
        fade = jnp.exp2(before[tile] * (-light_step * LOG2E))
        result.append(fade * (1.0 + 0.5 * jnp.tanh(slope)))
    return result


def shade_kernel(light_step, density_ref, ext_ref, shade_ref):
    light_cells, _, columns = density_ref.shape
    count = columns // LANES

    def layer(i, before):
        values = shaded(
            light_step,
            [density_ref[i, :, lanes(tile)] for tile in range(count)],
            before,
            lambda tile: density_ref[i - 1, :, lanes(tile)],
            lambda tile: density_ref[i + 1, :, lanes(tile)],
        )
        for tile in range(count):
            shade_ref[tile, eight(i)] = values[tile]
        return tuple(before[tile] + ext_ref[tile, eight(i)] for tile in range(count))

    for tile in range(count):
        shade_ref[tile, eight(0)] = jnp.zeros((8, LANES), F32)
        shade_ref[tile, eight(light_cells - 1)] = jnp.zeros((8, LANES), F32)
    before = tuple(ext_ref[tile, eight(0)] for tile in range(count))
    lax.fori_loop(1, light_cells - 1, layer, before, unroll=2)


def outer_kernel(light_step, light_count, density_ref, ext_ref, send_ref, pair_ref, edge_ref, _, shade_ref):
    light_cells, _, columns = density_ref.shape
    count = columns // LANES
    place = lax.axis_index("light")
    odd = lax.rem(place, 2) == 1
    inner = jnp.logical_and(place > 0, place < light_count - 1)
    last = light_cells - 1

    def beside(tile, pair_here):
        edge = jnp.where(inner, edge_ref[:, lanes(tile)], 0.0)
        return jnp.where(pair_here, pair_ref[1, :, lanes(tile)], edge)

    zero = jnp.zeros((8, LANES), F32)
    first = shaded(
        light_step, [density_ref[0, :, lanes(tile)] for tile in range(count)], [zero] * count,
        lambda tile: beside(tile, odd),
        lambda tile: density_ref[1, :, lanes(tile)],
    )
    for tile in range(count):
        shade_ref[tile, 0:8] = first[tile]
    final = shaded(
        light_step, [density_ref[last, :, lanes(tile)] for tile in range(count)],
        [send_ref[0, :, lanes(tile)] - ext_ref[tile, last * 8 : last * 8 + 8] for tile in range(count)],
        lambda tile: density_ref[last - 1, :, lanes(tile)],
        lambda tile: beside(tile, jnp.logical_not(odd)),
    )
    for tile in range(count):
        shade_ref[tile, last * 8 : last * 8 + 8] = final[tile]


def picture_kernel(light_step, tiles, masks, steps, shade_ref, term_ref, clear_ref, pair_ref, *refs):
    group_refs, out_refs, fade_ref = refs[: -len(steps) - 1], refs[-len(steps) - 1 : -1], refs[-1]
    _, depth_cells, light_cells, columns = term_ref.shape
    share = columns // tiles
    mine = lax.axis_index("tile")
    place = lax.axis_index("light")
    upstream = jnp.where((place & 1) > 0, pair_ref[0], 0.0)
    for mask, group_ref in zip(masks, group_refs):
        upstream = upstream + jnp.where((place ^ mask) < place, group_ref[...], 0.0)
    fade_ref[...] = jnp.exp2(upstream * (-light_step * LOG2E))
    for step, out_ref in zip(steps, out_refs):
        owner = lax.rem(mine + step, tiles)
        for tile in range(share // LANES):
            at = pl.ds(pl.multiple_of(owner * share + tile * LANES, LANES), LANES)
            for half in range(0, light_cells, 8):
                rows = slice(half, half + 8)
                sums = [jnp.zeros((8, LANES), F32) for _ in range(3)]
                for j in range(depth_cells):
                    fade = jnp.broadcast_to(fade_ref[j : j + 1, at], (8, LANES))
                    cells = pl.ds(half * depth_cells + j, 8, stride=depth_cells)
                    light = AMBIENT + fade * shade_ref[owner * (share // LANES) + tile, cells]
                    for c in range(3):
                        sums[c] = sums[c] + light * term_ref[c, j, rows, at]
                for c in range(3):
                    out_ref[c, rows, lanes(tile)] = sums[c]
                out_ref[3, rows, lanes(tile)] = clear_ref[rows, at]


def combine_kernel(front_ref, *refs):
    *in_refs, out_ref = refs
    steps = range(len(in_refs))
    _, light_cells, share = out_ref.shape
    for half in range(0, light_cells, 8):
        for tile in range(share // LANES):
            at = (slice(half, half + 8), lanes(tile))
            clear = [ref[3, *at] for ref in in_refs]
            sums = [jnp.zeros((8, LANES), F32) for _ in range(3)]
            through = clear[0]
            for step in steps[1:]:
                through = through * clear[step]
            for step in steps:
                ahead = jnp.ones((8, LANES), F32)
                for other in steps:
                    if other != step:
                        ahead = ahead * jnp.where(front_ref[step * len(steps) + other] > 0.5, clear[other], 1.0)
                for c in range(3):
                    sums[c] = sums[c] + ahead * in_refs[step][c, *at]
            for c in range(3):
                out_ref[c, *at] = sums[c]
            out_ref[3, *at] = 1.0 - through


def call(kernel, outs, ins, name, scratch=(), cost=1.0, aliases=None):
    cycles = int(cost * 1000)
    return pl.pallas_call(
        kernel,
        out_shape=outs,
        in_specs=[pl.BlockSpec(memory_space=pltpu.VMEM)] * len(ins),
        out_specs=jax.tree.map(lambda _: pl.BlockSpec(memory_space=pltpu.VMEM), outs),
        scratch_shapes=list(scratch),
        compiler_params=pltpu.CompilerParams(vmem_limit_bytes=8 * 2**20),
        cost_estimate=pl.CostEstimate(flops=cycles * 1000, bytes_accessed=cycles * 3000, transcendentals=0),
        input_output_aliases=aliases or {},
        name=name,
    )(*ins)


def per_device(density, bin_index, transfer, depth_order):
    light_cells, depth_cells, columns = density.shape
    light_count = lax.axis_size("light")
    tile_count = lax.axis_size("tile")
    light_step = 3.0 / (light_cells * light_count)
    view_step = 3.0 / (depth_cells * tile_count)
    share = columns // tile_count

    def shape(*dims, dtype=F32):
        return jax.ShapeDtypeStruct(dims, dtype)

    plane = shape(depth_cells, columns)
    tiled = (columns // LANES, light_cells * depth_cells, LANES)
    hbm = pl.BlockSpec(memory_space=pltpu.HBM)
    vmem = pl.BlockSpec(memory_space=pltpu.VMEM)
    outs = [
        shape(*density.shape), shape(*transfer.shape), shape(*tiled, dtype=jnp.int32), shape(*tiled),
        shape(2, *plane.shape), plane, shape(tile_count * tile_count, 8, LANES),
    ]
    dense, table, entry, ext, send, edge, front = pl.pallas_call(
        functools.partial(extinction_kernel, tile_count),
        out_shape=outs,
        in_specs=[hbm] * 4,
        out_specs=[vmem] * len(outs),
        scratch_shapes=[
            pltpu.VMEM(bin_index.shape, jnp.int32),
            pltpu.SMEM(depth_order.shape, jnp.int32),
            pltpu.SemaphoreType.DMA((2,)),
            pltpu.SemaphoreType.DMA((2,)),
            pltpu.SemaphoreType.DMA,
            pltpu.SemaphoreType.DMA,
        ],
        compiler_params=pltpu.CompilerParams(vmem_limit_bytes=8 * 2**20),
        name="extinction",
    )(*[pltpu.with_memory_space_constraint(a, pltpu.HBM) for a in (density, bin_index, transfer, depth_order)])

    pair = lax.ppermute(send, "light", [(i, i ^ 1) for i in range(light_count)])
    beside = [(i, (i + 1) % light_count) for i in range(1, light_count, 2)]
    edge = lax.ppermute(edge, "light", beside + [(b, a) for a, b in beside])
    term, clear = call(
        functools.partial(terms_kernel, view_step),
        [shape(3, depth_cells, light_cells, columns), shape(light_cells, columns)],
        (table, entry, ext), "terms", cost=2.5,
    )
    shade = call(
        functools.partial(shade_kernel, light_step), shape(*tiled), (dense, ext), "shade", cost=1.2
    )
    group = send[0] + pair[0]
    groups = []
    masks = []
    step = 2
    while step < light_count:
        reach = [m * step for m in (1, 2, 3)] if step * 4 <= light_count else [step]
        got = [lax.ppermute(group, "light", [(i, i ^ m) for i in range(light_count)]) for m in reach]
        groups += got
        masks += reach
        group = group + functools.reduce(jnp.add, got)
        step *= len(reach) + 1
    shade = call(
        functools.partial(outer_kernel, light_step, light_count), shape(*tiled),
        (dense, ext, send, pair, edge, shade), "outer", cost=0.2, aliases={5: 0},
    )
    held = {}
    for steps in ([1], [*range(2, tile_count)], [0]):
        pieces = call(
            functools.partial(picture_kernel, light_step, tile_count, masks, steps),
            [shape(4, light_cells, share)] * len(steps),
            (shade, term, clear, pair, *groups), "picture",
            scratch=[pltpu.VMEM(plane.shape, F32)], cost=0.2 * len(steps),
        )
        for step, piece in zip(steps, pieces):
            held[step] = piece
            if step:
                held[step] = lax.ppermute(piece, "tile", [(i, (i + step) % tile_count) for i in range(tile_count)])
    return call(
        combine_kernel, shape(4, light_cells, share), (front, *[held[step] for step in range(tile_count)]), "combine"
    )


def solution(mesh):
    in_specs = (P("light", "tile", None), P("light", "tile", None), P(), P())
    out_specs = P(None, "light", "tile")
    return jax.shard_map(
        per_device, mesh=mesh, in_specs=in_specs, out_specs=out_specs, check_vma=False
    )
```
